32 devices in a mesh: outer: 8 (over z, core), inner: 4 (over y, x).
Axes of the slice: x: 2, y: 2, z: 4, core: 2. Of those that a mesh axis runs over, the one named last changes fastest.
Arguments:
- queries: bfloat16 [8, 4096, 128], P(None, ('outer', 'inner')), may hold values from -6 to 6
- key_states: bfloat16 [4096, 128], P(('outer', 'inner')), may hold values from -6 to 6
- value_states: bfloat16 [4096, 128], P(('outer', 'inner')), may hold values from -6 to 6
- outputs: bfloat16 [8, 4096, 128], P(None, ('outer', 'inner')), may hold values from -6 to 6
- grad_outputs: bfloat16 [8, 4096, 128], P(None, ('outer', 'inner')), may hold values from -6 to 6
- log_sums: float32 [8, 4096], P(None, ('outer', 'inner')), may hold values from -1 to 20
- span_order: int32 [64], replicated, may hold values from 0 to 63, as said below
Outputs:
- query_grads: bfloat16 [8, 4096, 128], P(None, ('outer', 'inner'))
- key_grads: bfloat16 [4096, 128], P(('outer', 'inner'))
- value_grads: bfloat16 [4096, 128], P(('outer', 'inner'))
The draws below stay inside these ranges and needn't reach their ends.
Inputs may be any that keep to these rules, and one draw needn't show every extreme that they name: span_order is a permutation of the 64 position blocks; entries 2 d and 2 d + 1 (the blocks stored on device d) add up to 63.
All inputs are finite; a program needn't handle non-finite values.
Results may differ from the reference program's by a relative error of at most 0.0052.
Values may be sent and summed in bfloat16 or wider, within the bound.
A program may use at most 64 MiB of HBM per device.

```python
import math
import jax
import jax.numpy as jnp
from jax import lax

DH = 128
H = 8
SPAN = 64
BLOCKS = 64
TOKENS = 4096


def block_order(key):
    order_key = jax.random.fold_in(key, 11)
    half_blocks = BLOCKS // 2
    chosen = jax.random.permutation(jax.random.fold_in(order_key, 1), half_blocks).astype(jnp.int32)
    flips = jax.random.randint(jax.random.fold_in(order_key, 2), (half_blocks,), 0, 2).astype(jnp.int32)
    first_block = jnp.where(flips == 1, BLOCKS - 1 - chosen, chosen)
    second_block = BLOCKS - 1 - first_block
    return jnp.stack([first_block, second_block], axis=1).reshape(BLOCKS).astype(jnp.int32)


def draw_span_order(key, part):
    return block_order(key)


def draw_log_sums(key, part):
    order = block_order(key)
    row_ids = jnp.arange(TOKENS, dtype=jnp.int32)
    seq_pos = order[row_ids // SPAN] * SPAN + row_ids % SPAN
    baseline = jnp.log(seq_pos.astype(jnp.float32) + 1.0)
    noise_key = jax.random.fold_in(key, 23)
    offsets = jax.random.uniform(noise_key, (H, TOKENS), jnp.float32, 0.2, 0.8)
    return baseline[None, :] + offsets


def levels(key, extent, shards, smallest, largest):
    def one(dim, blocks):
        heights = jax.random.uniform(jax.random.fold_in(jax.random.fold_in(key, 6), dim), (blocks,), jnp.float32, smallest / len(shards), largest / len(shards))
        return jnp.repeat(jnp.exp(heights), extent[dim] // blocks).reshape((-1,) + (1,) * (len(extent) - dim - 1))

    loudness = one(*shards[0])
    for cut in shards[1:]:
        loudness = loudness * one(*cut)
    return loudness


def noise(stream_key, extent, spread, reach, cuts=(), held_as=jnp.bfloat16):
    gain = levels(stream_key, extent, cuts, -0.22, 0.18) if cuts else 1.0
    result = jax.random.normal(stream_key, extent, jnp.float32) * spread * gain
    return jnp.minimum(jnp.maximum(result, -reach), reach).astype(held_as)


def setup_inputs(seed: int = 0) -> dict:
    seeds = jax.random.split(jax.random.key(seed), 8)
    queries = noise(seeds[0], (H, TOKENS, DH), 1.0, 6.0, ((1, 32),))
    key_states = noise(seeds[1], (TOKENS, DH), 1.0, 6.0, ((0, 32),))
    value_states = noise(seeds[2], (TOKENS, DH), 1.0, 6.0, ((0, 32),))
    outputs = noise(seeds[3], (H, TOKENS, DH), 1.0, 6.0, ((1, 32),))
    grad_outputs = noise(seeds[4], (H, TOKENS, DH), 1.0, 6.0, ((1, 32),))
    log_sums = draw_log_sums(jax.random.fold_in(seeds[7], 71), 0)
    span_order = draw_span_order(jax.random.fold_in(seeds[7], 71), 0)
    return {"queries": queries, "key_states": key_states, "value_states": value_states, "outputs": outputs, "grad_outputs": grad_outputs, "log_sums": log_sums, "span_order": span_order}


def positions(span_order):
    row_ids = jnp.arange(TOKENS, dtype=jnp.int32)
    return (span_order[row_ids // SPAN] * SPAN + row_ids % SPAN).astype(jnp.int32)

def reference(queries, key_states, value_states, outputs, grad_outputs, log_sums, span_order):
    softmax_scale = 1.0 / math.sqrt(DH)
    seq_pos = positions(span_order)
    deltas = lax.optimization_barrier(jnp.sum(grad_outputs.astype(jnp.float32) * outputs.astype(jnp.float32), axis=-1))
    query_block = math.gcd(256, TOKENS)
    block_count = TOKENS // query_block

    def one_block(carried, block_index):
        grad_keys, grad_values = carried
        first_row = (block_index * query_block).astype(jnp.int32)
        query_rows = lax.dynamic_slice_in_dim(queries, first_row, query_block, 1).reshape(H * query_block, DH)
        grad_rows = lax.dynamic_slice_in_dim(grad_outputs, first_row, query_block, 1).reshape(H * query_block, DH)
        log_norm = lax.dynamic_slice_in_dim(log_sums, first_row, query_block, 1).reshape(H * query_block, 1)
        delta_rows = lax.dynamic_slice_in_dim(deltas, first_row, query_block, 1).reshape(H * query_block, 1)
        query_pos = jnp.tile(lax.dynamic_slice_in_dim(seq_pos, first_row, query_block, 0), H)
        scores = jnp.dot(query_rows, key_states.T, preferred_element_type=jnp.float32) * softmax_scale
        visible = query_pos[:, None] >= seq_pos[None, :]
        attend = jnp.where(visible, jnp.exp(scores - log_norm), jnp.float32(0.0))
        grad_prob = jnp.dot(grad_rows, value_states.T, preferred_element_type=jnp.float32)
        grad_score = attend * (grad_prob - delta_rows)
        attend_low = attend.astype(jnp.bfloat16)
        score_low = grad_score.astype(jnp.bfloat16)
        grad_values = grad_values + jnp.dot(attend_low.T, grad_rows, preferred_element_type=jnp.float32)
        grad_keys = grad_keys + jnp.dot(score_low.T, query_rows, preferred_element_type=jnp.float32) * softmax_scale
        grad_query = jnp.dot(score_low, key_states, preferred_element_type=jnp.float32) * softmax_scale
        return ((grad_keys, grad_values), grad_query.astype(jnp.bfloat16).reshape(H, query_block, DH))
    initial = (jnp.zeros((TOKENS, DH), jnp.float32), jnp.zeros((TOKENS, DH), jnp.float32))
    (grad_keys, grad_values), pieces = lax.scan(one_block, initial, jnp.arange(block_count, dtype=jnp.int32))
    query_grads = jnp.transpose(pieces, (1, 0, 2, 3)).reshape(H, TOKENS, DH)
    return (query_grads, grad_keys.astype(jnp.bfloat16), grad_values.astype(jnp.bfloat16))
```

```python
import functools
import math

import jax
import jax.numpy as jnp
from jax import lax
from jax.experimental import pallas as pl
from jax.experimental.pallas import tpu as pltpu
from jax.sharding import PartitionSpec as P

MESH = pl.DeviceIdType.MESH
F32 = jnp.float32
BF16 = jnp.bfloat16
LOG2E = math.log2(math.e)


def dot(a, b, dims, precision=None):
    return lax.dot_general(
        a, b, ((dims[:1], dims[1:]), ((), ())), precision=precision, preferred_element_type=F32
    )


def kernel(
    planes, inner,
    order, q_ref, k_ref, v_ref, o_ref, g_ref, lse_ref,
    dq_out, dk_out, dv_out,
    kv, q2, g2, stats, low_pos, dq_acc, dq_send, dq_recv,
    diag, full, own, part_send, part_recv, z_send, z_recv,
    s_outer, s_inner, r_kv, s_q, r_q, s_part, r_part, s_z, r_z, s_dq, r_dq,
):
    heads, rows, width = q_ref.shape
    span = rows // 2
    cols = heads * span
    scale = 1.0 / math.sqrt(width)
    outer_id = lax.axis_index("outer")
    i = lax.axis_index("inner")
    core = lax.rem(outer_id, 2)
    z = outer_id // 2
    partner = (outer_id + 1 - 2 * core, i)

    def plane_of(step):
        return lax.rem(z + step, planes)

    def peer_of(step):
        return lax.rem(i + step, inner)

    def column(plane):
        return (plane * 2 + core, i)

    def beside(peer):
        return (outer_id, peer)

    def rank(plane, peer):
        return (plane * 2 + core) * inner + peer

    barrier = pltpu.get_barrier_semaphore()
    for step in range(1, planes):
        pl.semaphore_signal(barrier, inc=1, device_id=column(plane_of(step)), device_id_type=MESH)
    for step in range(1, inner):
        pl.semaphore_signal(barrier, inc=1, device_id=beside(peer_of(step)), device_id_type=MESH)
    pl.semaphore_signal(barrier, inc=1, device_id=partner, device_id_type=MESH)

    my_rank = outer_id * inner + i
    first = order[2 * my_rank]
    second = order[2 * my_rank + 1]

    def ordered(a, b):
        shape = a.shape
        straight = jnp.full(shape, first, jnp.int32) < jnp.full(shape, second, jnp.int32)
        a, b = a.astype(F32), b.astype(F32)
        return jnp.where(straight, a, b), jnp.where(straight, b, a)

    my_low = jnp.minimum(first, second)
    other_rank = partner[0] * inner + i
    other_low = jnp.minimum(order[2 * other_rank], order[2 * other_rank + 1])

    def kv_slot(plane, peer):
        return kv.at[plane, :, pl.ds(pl.multiple_of(peer * span, span), span), :]

    k_low, k_high = (x.astype(BF16) for x in ordered(k_ref[:span, :], k_ref[span:, :]))
    v_low, v_high = (x.astype(BF16) for x in ordered(v_ref[:span, :], v_ref[span:, :]))
    mine = pl.ds(pl.multiple_of(i * span, span), span)
    kv[z, 0, mine, :width] = k_low
    kv[z, 0, mine, width:] = v_low
    kv[z, 1, mine, :width] = k_high
    kv[z, 1, mine, width:] = v_high

    pl.semaphore_wait(barrier, planes + inner - 1)

    def send_column(step):
        return pltpu.make_async_remote_copy(
            src_ref=kv_slot(z, i), dst_ref=kv_slot(z, i),
            send_sem=s_outer.at[step], recv_sem=r_kv.at[z, i],
            device_id=column(plane_of(step)), device_id_type=MESH,
        )

    def send_beside(plane, step):
        return pltpu.make_async_remote_copy(
            src_ref=kv_slot(plane, i), dst_ref=kv_slot(plane, i),
            send_sem=s_inner.at[plane, step], recv_sem=r_kv.at[plane, i],
            device_id=beside(peer_of(step)), device_id_type=MESH,
        )

    def wait_kv(plane, peer):
        pltpu.make_async_remote_copy(
            src_ref=kv_slot(plane, peer), dst_ref=kv_slot(plane, peer),
            send_sem=s_outer.at[0], recv_sem=r_kv.at[plane, peer],
            device_id=partner, device_id_type=MESH,
        ).wait_recv()

    for step in range(1, planes):
        send_column(step).start()
    for step in range(1, inner):
        send_beside(z, step).start()

    def flat(ref):
        first_part = ref[:, :span, :].reshape(cols, width)
        return ordered(first_part, ref[:, span:, :].reshape(cols, width))

    g_wide = flat(g_ref)
    g_low, g_high = (x.astype(BF16) for x in g_wide)
    g2[0, :, :width] = g_low
    g2[0, :, width:] = g_high
    q_low, q_high = (x.astype(BF16) for x in flat(q_ref))
    q2[0, :, :width] = q_low
    q2[0, :, width:] = q_high

    def exchange(ref, index):
        return pltpu.make_async_remote_copy(
            src_ref=ref.at[0], dst_ref=ref.at[1], send_sem=s_q.at[index], recv_sem=r_q.at[index],
            device_id=partner, device_id_type=MESH,
        )

    exchange(q2, 0).start()
    exchange(g2, 1).start()
    ones = jnp.ones((8, width), F32)
    lse_first = jnp.concatenate([lse_ref[h : h + 1, :span] for h in range(heads)], axis=1) * LOG2E
    lse_second = jnp.concatenate([lse_ref[h : h + 1, span:] for h in range(heads)], axis=1) * LOG2E
    stats[0, 0:1, :], stats[0, 1:2, :] = ordered(lse_first, lse_second)
    for at, g_part, o_part in zip((2, 3), g_wide, flat(o_ref)):
        product = g_part * o_part
        stats[0, at : at + 1, :] = dot(ones, product, (1, 1), lax.Precision.HIGHEST)[0:1]
    stats[0, 4:8, :] = jnp.zeros((4, cols), F32)
    exchange(stats, 2).start()

    for step in range(1, planes):
        plane = plane_of(step)
        wait_kv(plane, i)
        for hop in range(1, inner):
            send_beside(plane, hop).start()

    key_row = lax.broadcasted_iota(jnp.int32, (span, cols), 0)
    query_row = lax.rem(lax.broadcasted_iota(jnp.int32, (span, cols), 1), span)
    visible = query_row >= key_row
    for half, k_part, v_part, q_part, g_part in (
        (0, k_low, v_low, q_low, g_low), (1, k_high, v_high, q_high, g_high),
    ):
        scores = dot(k_part, q_part, (1, 1)) * (scale * LOG2E)
        attend = jnp.where(visible, jnp.exp2(scores - stats[0, half : half + 1, :]), 0.0)
        grad = dot(v_part, g_part, (1, 1)) - stats[0, 2 + half : 3 + half, :]
        score_low = (attend * grad).astype(BF16)
        diag[half, :, :width] = dot(score_low, q_part, (1, 0))
        diag[half, :, width:] = dot(attend.astype(BF16), g_part, (1, 0))
        dq_acc[0, half * width : (half + 1) * width, :] = dot(k_part, score_low, (0, 0))
    dq_acc[1] = jnp.zeros((2 * width, cols), F32)

    for plane in range(planes):
        for peer in range(inner):
            at = 2 * rank(plane, peer)
            low = jnp.minimum(order[at], order[at + 1])
            low_pos[plane, peer * span : (peer + 1) * span, :] = jnp.full((span, width), low, jnp.int32)

    for index, ref in enumerate((q2, g2, stats)):
        exchange(ref, index).wait_recv()

    def send_part(plane, step):
        peer = peer_of(step)
        return pltpu.make_async_remote_copy(
            src_ref=part_send.at[plane, :, pl.ds(pl.multiple_of(peer * span, span), span), :],
            dst_ref=part_recv.at[plane, i],
            send_sem=s_part.at[plane, step], recv_sem=r_part.at[plane, i],
            device_id=beside(peer), device_id_type=MESH,
        )

    def gather_part(plane):
        total = own[plane]
        for step in range(1, inner):
            peer = peer_of(step)
            pltpu.make_async_remote_copy(
                src_ref=part_recv.at[plane, peer], dst_ref=part_recv.at[plane, peer],
                send_sem=s_part.at[plane, 0], recv_sem=r_part.at[plane, peer],
                device_id=partner, device_id_type=MESH,
            ).wait_recv()
            total = total + part_recv[plane, peer].astype(F32)
        return total

    def send_plane(step):
        plane = plane_of(step)
        return pltpu.make_async_remote_copy(
            src_ref=z_send.at[plane], dst_ref=z_recv.at[z],
            send_sem=s_z.at[step], recv_sem=r_z.at[z],
            device_id=column(plane), device_id_type=MESH,
        )

    def pass_on(step):
        plane = plane_of(step)
        z_send[plane] = gather_part(plane).astype(BF16)
        send_plane(step).start()

    def one_plane(step, carried):
        plane = plane_of(step)
        for hop in range(1, inner):
            wait_kv(plane, peer_of(hop))
        k_l, v_l = kv[plane, 0, :, :width], kv[plane, 0, :, width:]
        k_h, v_h = kv[plane, 1, :, :width], kv[plane, 1, :, width:]
        pos = low_pos[plane]
        wide_pos = jnp.concatenate([pos] * (cols // width), axis=1)
        dk_l = dv_l = dk_h = dv_h = None
        for j, edge in ((0, my_low), (1, other_low)):
            def below(x):
                return jnp.where(pos < edge, x, 0.0)

            def above(x):
                return jnp.where(pos > edge, x, 0.0)

            def chosen(low, high):
                low, high = below(low.astype(F32)), above(high.astype(F32))
                return jnp.concatenate([low.astype(BF16), high.astype(BF16)], axis=1)

            q_both, g_both = q2[j], g2[j]
            q_h, g_h = q_both[:, width:], g_both[:, width:]
            lse_l, lse_h = stats[j, 0:1, :], stats[j, 1:2, :]
            del_l, del_h = stats[j, 2:3, :], stats[j, 3:4, :]
            attend = jnp.exp2(dot(k_l, q_h, (1, 1)) * (scale * LOG2E) - lse_h)
            score_low = (attend * (dot(v_l, g_h, (1, 1)) - del_h)).astype(BF16)
            dv1 = dot(attend.astype(BF16), g_h, (1, 0))
            dk1 = dot(score_low, q_h, (1, 0))
            dq_acc[j, width:, :] += dot(k_l, score_low, (0, 0))
            is_below = wide_pos < edge
            k_c, v_c = chosen(k_l, k_h), chosen(v_l, v_h)
            attend = jnp.exp2(
                dot(k_c, q_both, (1, 1)) * (scale * LOG2E) - jnp.where(is_below, lse_l, lse_h)
            )
            grad = dot(v_c, g_both, (1, 1)) - jnp.where(is_below, del_l, del_h)
            score_low = (attend * grad).astype(BF16)
            dv2 = dot(attend.astype(BF16), g_both, (1, 0))
            dk2 = dot(score_low, q_both, (1, 0))
            dq_acc[j] += dot(k_c, score_low, (0, 0))
            dk_lj, dk_hj = dk1 + below(dk2[:, :width]), above(dk2[:, width:])
            dv_lj, dv_hj = dv1 + below(dv2[:, :width]), above(dv2[:, width:])
            if j == 0:
                dk_l, dk_h, dv_l, dv_h = dk_lj, dk_hj, dv_lj, dv_hj
            else:
                dk_l, dk_h, dv_l, dv_h = dk_l + dk_lj, dk_h + dk_hj, dv_l + dv_lj, dv_h + dv_hj
        for half, dk, dv in ((0, dk_l, dv_l), (1, dk_h, dv_h)):
            full[half, :, :width] = dk
            full[half, :, width:] = dv
            part_send[plane, half, :, :width] = dk.astype(BF16)
            part_send[plane, half, :, width:] = dv.astype(BF16)
        own[plane] = full[:, mine, :]
        for hop in range(1, inner):
            send_part(plane, hop).start()

        @pl.when(step >= 2)
        def _():
            pass_on(step - 1)

        return carried

    lax.fori_loop(0, planes, one_plane, 0)

    dq_send[...] = dq_acc[1].astype(BF16)
    dq_copy = pltpu.make_async_remote_copy(
        src_ref=dq_send, dst_ref=dq_recv, send_sem=s_dq, recv_sem=r_dq,
        device_id=partner, device_id_type=MESH,
    )
    dq_copy.start()
    pass_on(planes - 1)

    dq_copy.wait_recv()
    dq = (dq_acc[0] + dq_recv[...].astype(F32)) * scale
    for at, part in zip((0, span), ordered(dq[:width], dq[width:])):
        dq_out[:, at : at + span, :] = part.T.astype(BF16).reshape(heads, span, width)

    total = gather_part(z) + diag[...]
    for step in range(1, planes):
        plane = plane_of(step)
        pltpu.make_async_remote_copy(
            src_ref=z_recv.at[plane], dst_ref=z_recv.at[plane],
            send_sem=s_z.at[0], recv_sem=r_z.at[plane],
            device_id=partner, device_id_type=MESH,
        ).wait_recv()
        total = total + z_recv[plane].astype(F32)
    for at, part in zip((0, span), ordered(total[0], total[1])):
        dk_out[at : at + span, :] = (part[:, :width] * scale).astype(BF16)
        dv_out[at : at + span, :] = part[:, width:].astype(BF16)

    for step in range(1, planes):
        send_column(step).wait_send()
        send_plane(step).wait_send()
    for step in range(planes):
        for hop in range(1, inner):
            send_beside(plane_of(step), hop).wait_send()
            send_part(plane_of(step), hop).wait_send()
    for index, ref in enumerate((q2, g2, stats)):
        exchange(ref, index).wait_send()
    dq_copy.wait_send()


def body(queries, key_states, value_states, outputs, grad_outputs, log_sums, span_order):
    heads, rows, width = queries.shape
    planes = lax.axis_size("outer") // 2
    inner = lax.axis_size("inner")
    span = rows // 2
    cols = heads * span
    group = inner * span
    vmem = pl.BlockSpec(memory_space=pltpu.VMEM)
    dma = pltpu.SemaphoreType.DMA
    return pl.pallas_call(
        functools.partial(kernel, planes, inner),
        out_shape=(
            jax.ShapeDtypeStruct(queries.shape, BF16),
            jax.ShapeDtypeStruct(key_states.shape, BF16),
            jax.ShapeDtypeStruct(value_states.shape, BF16),
        ),
        in_specs=[pl.BlockSpec(memory_space=pltpu.SMEM)] + [vmem] * 6,
        out_specs=(vmem, vmem, vmem),
        scratch_shapes=[
            pltpu.VMEM((planes, 2, group, 2 * width), BF16),
            pltpu.VMEM((2, cols, 2 * width), BF16),
            pltpu.VMEM((2, cols, 2 * width), BF16),
            pltpu.VMEM((2, 8, cols), F32),
            pltpu.VMEM((planes, group, width), jnp.int32),
            pltpu.VMEM((2, 2 * width, cols), F32),
            pltpu.VMEM((2 * width, cols), BF16),
            pltpu.VMEM((2 * width, cols), BF16),
            pltpu.VMEM((2, span, 2 * width), F32),
            pltpu.VMEM((2, group, 2 * width), F32),
            pltpu.VMEM((planes, 2, span, 2 * width), F32),
            pltpu.VMEM((planes, 2, group, 2 * width), BF16),
            pltpu.VMEM((planes, inner, 2, span, 2 * width), BF16),
            pltpu.VMEM((planes, 2, span, 2 * width), BF16),
            pltpu.VMEM((planes, 2, span, 2 * width), BF16),
            dma((planes,)), dma((planes, inner)), dma((planes, inner)),
            dma((3,)), dma((3,)),
            dma((planes, inner)), dma((planes, inner)),
            dma((planes,)), dma((planes,)),
            dma, dma,
        ],
        compiler_params=pltpu.CompilerParams(
            collective_id=0, has_side_effects=True, vmem_limit_bytes=48 * 1024 * 1024
        ),
        cost_estimate=pl.CostEstimate(
            flops=10 * 65 * cols * span * width * planes * inner // 16,
            bytes_accessed=4 * heads * rows * width * 2,
            transcendentals=0,
        ),
    )(span_order, queries, key_states, value_states, outputs, grad_outputs, log_sums)


def solution(mesh):
    return jax.shard_map(
        body,
        mesh=mesh,
        in_specs=(
            P(None, ("outer", "inner"), None),
            P(("outer", "inner"), None),
            P(("outer", "inner"), None),
            P(None, ("outer", "inner"), None),
            P(None, ("outer", "inner"), None),
            P(None, ("outer", "inner")),
            P(),
        ),
        out_specs=(
            P(None, ("outer", "inner"), None),
            P(("outer", "inner"), None),
            P(("outer", "inner"), None),
        ),
        check_vma=False,
    )
```

```python
import functools
import math

import jax
import jax.numpy as jnp
from jax import lax
from jax.experimental import pallas as pl
from jax.experimental.pallas import tpu as pltpu
from jax.sharding import PartitionSpec as P

MESH = pl.DeviceIdType.MESH
F32 = jnp.float32
BF16 = jnp.bfloat16
LOG2E = math.log2(math.e)


def dot(a, b, dims, precision=None):
    return lax.dot_general(
        a, b, ((dims[:1], dims[1:]), ((), ())), precision=precision, preferred_element_type=F32
    )


def kernel(
    planes, inner,
    order_hbm, q_hbm, k_hbm, v_hbm, o_hbm, g_hbm, lse_hbm,
    dq_out, dk_out, dv_out,
    kv, q2, g2, stats, low_pos, dq_acc, dq_send, dq_recv,
    diag, full, own, part_send, part_recv, z_send, z_recv,
    order, q_ref, k_ref, v_ref, o_ref, g_ref, lse_ref, loads,
    s_outer, s_inner, r_kv, s_cross, r_cross, s_q, r_q, s_part, r_part, s_z, r_z, s_dq, r_dq,
):
    heads, rows, width = q_ref.shape
    span = rows // 2
    cols = heads * span
    scale = 1.0 / math.sqrt(width)
    outer_id = lax.axis_index("outer")
    i = lax.axis_index("inner")
    core = lax.rem(outer_id, 2)
    z = outer_id // 2
    partner = (outer_id + 1 - 2 * core, i)

    def plane_of(step):
        if planes & (planes - 1):
            return lax.rem(z + step, planes)
        plane, bit = 0, 1
        while bit < planes:
            plane = plane + bit * lax.rem(lax.div(z, bit) + lax.div(jnp.int32(step), jnp.int32(bit)), 2)
            bit *= 2
        return plane

    side = lax.rem(i, 2)
    across = i + 1 - 2 * side
    along = [2 * lax.rem(i // 2 + t, inner // 2) + side for t in range(inner // 2)]
    cross = [peer + 1 - 2 * side for peer in along]

    def peer_of(step):
        return lax.rem(i + step, inner)

    def column(plane):
        return (plane * 2 + core, i)

    def beside(peer):
        return (outer_id, peer)

    def rank(plane, peer):
        return (plane * 2 + core) * inner + peer

    staged = (
        (order_hbm, order), (k_hbm, k_ref), (v_hbm, v_ref), (g_hbm, g_ref), (q_hbm, q_ref),
        (lse_hbm, lse_ref), (o_hbm, o_ref),
    )
    fetch = [pltpu.make_async_copy(a, b, loads.at[n]) for n, (a, b) in enumerate(staged)]
    for one in fetch:
        one.start()

    barrier = pltpu.get_barrier_semaphore()
    for step in range(1, planes):
        pl.semaphore_signal(barrier, inc=1, device_id=column(plane_of(step)), device_id_type=MESH)
    for step in range(1, inner):
        pl.semaphore_signal(barrier, inc=1, device_id=beside(peer_of(step)), device_id_type=MESH)
    pl.semaphore_signal(barrier, inc=1, device_id=partner, device_id_type=MESH)

    for one in fetch[:3]:
        one.wait()
    my_rank = outer_id * inner + i
    first = order[2 * my_rank]
    second = order[2 * my_rank + 1]

    def ordered(a, b):
        shape = a.shape
        straight = jnp.full(shape, first, jnp.int32) < jnp.full(shape, second, jnp.int32)
        a, b = a.astype(F32), b.astype(F32)
        return jnp.where(straight, a, b), jnp.where(straight, b, a)

    my_low = jnp.minimum(first, second)
    other_rank = partner[0] * inner + i
    other_low = jnp.minimum(order[2 * other_rank], order[2 * other_rank + 1])

    def kv_slot(plane, peer):
        return kv.at[plane, :, pl.ds(pl.multiple_of(peer * span, span), span), :]

    k_low, k_high = (x.astype(BF16) for x in ordered(k_ref[:span, :], k_ref[span:, :]))
    v_low, v_high = (x.astype(BF16) for x in ordered(v_ref[:span, :], v_ref[span:, :]))
    mine = pl.ds(pl.multiple_of(i * span, span), span)
    kv[z, 0, mine, :width] = k_low
    kv[z, 0, mine, width:] = v_low
    kv[z, 1, mine, :width] = k_high
    kv[z, 1, mine, width:] = v_high

    pl.semaphore_wait(barrier, planes + inner - 1)

    def send_column(step):
        return pltpu.make_async_remote_copy(
            src_ref=kv_slot(z, i), dst_ref=kv_slot(z, i),
            send_sem=s_outer.at[step], recv_sem=r_kv.at[z, i],
            device_id=column(plane_of(step)), device_id_type=MESH,
        )

    def send_beside(plane, t):
        return pltpu.make_async_remote_copy(
            src_ref=kv_slot(plane, i), dst_ref=kv_slot(plane, i),
            send_sem=s_inner.at[plane, t], recv_sem=r_kv.at[plane, i],
            device_id=beside(along[t] if t else across), device_id_type=MESH,
        )

    def half_slot(plane, peer, half):
        return kv.at[plane, half, pl.ds(pl.multiple_of(peer * span, span), span), :]

    def send_cross(plane, t, half):
        source, target = (across, along[t]) if half == 0 else (along[t], across)
        return pltpu.make_async_remote_copy(
            src_ref=half_slot(plane, source, half), dst_ref=half_slot(plane, source, half),
            send_sem=s_cross.at[plane, t, half], recv_sem=r_cross.at[plane, source, half],
            device_id=beside(target), device_id_type=MESH,
        )

    def wait_kv(plane, peer):
        pltpu.make_async_remote_copy(
            src_ref=kv_slot(plane, peer), dst_ref=kv_slot(plane, peer),
            send_sem=s_outer.at[0], recv_sem=r_kv.at[plane, peer],
            device_id=partner, device_id_type=MESH,
        ).wait_recv()

    def wait_cross(plane, peer, half):
        pltpu.make_async_remote_copy(
            src_ref=half_slot(plane, peer, half), dst_ref=half_slot(plane, peer, half),
            send_sem=s_outer.at[0], recv_sem=r_cross.at[plane, peer, half],
            device_id=partner, device_id_type=MESH,
        ).wait_recv()

    rows_of = range(1, inner // 2)

    def spread(plane):
        for t in range(inner // 2):
            send_beside(plane, t).start()

    def forward(plane):
        wait_kv(plane, across)
        for t in rows_of:
            send_cross(plane, t, 0).start()
        for t in rows_of:
            wait_kv(plane, along[t])
            send_cross(plane, t, 1).start()

    for step in range(1, planes):
        send_column(step).start()
    spread(z)

    def flat(ref):
        first_part = ref[:, :span, :].reshape(cols, width)
        return ordered(first_part, ref[:, span:, :].reshape(cols, width))

    fetch[3].wait()
    g_wide = flat(g_ref)
    g_low, g_high = (x.astype(BF16) for x in g_wide)
    g2[0, :, :width] = g_low
    g2[0, :, width:] = g_high
    fetch[4].wait()
    q_low, q_high = (x.astype(BF16) for x in flat(q_ref))
    q2[0, :, :width] = q_low
    q2[0, :, width:] = q_high

    def exchange(ref, index):
        return pltpu.make_async_remote_copy(
            src_ref=ref.at[0], dst_ref=ref.at[1], send_sem=s_q.at[index], recv_sem=r_q.at[index],
            device_id=partner, device_id_type=MESH,
        )

    exchange(q2, 0).start()
    exchange(g2, 1).start()
    fetch[5].wait()
    fetch[6].wait()
    ones = jnp.ones((8, width), F32)
    lse_first = jnp.concatenate([lse_ref[h : h + 1, :span] for h in range(heads)], axis=1) * LOG2E
    lse_second = jnp.concatenate([lse_ref[h : h + 1, span:] for h in range(heads)], axis=1) * LOG2E
    stats[0, 0:1, :], stats[0, 1:2, :] = ordered(lse_first, lse_second)
    for at, g_part, o_part in zip((2, 3), g_wide, flat(o_ref)):
        product = g_part * o_part
        stats[0, at : at + 1, :] = dot(ones, product, (1, 1), lax.Precision.HIGHEST)[0:1]
    stats[0, 4:8, :] = jnp.zeros((4, cols), F32)
    exchange(stats, 2).start()

    for step in range(1, planes):
        wait_kv(plane_of(step), i)
        spread(plane_of(step))
        if step == 1:
            forward(z)

    key_row = lax.broadcasted_iota(jnp.int32, (span, cols), 0)
    query_row = lax.rem(lax.broadcasted_iota(jnp.int32, (span, cols), 1), span)
    visible = query_row >= key_row
    for half, k_part, v_part, q_part, g_part in (
        (0, k_low, v_low, q_low, g_low), (1, k_high, v_high, q_high, g_high),
    ):
        scores = dot(k_part, q_part, (1, 1)) * (scale * LOG2E)
        attend = jnp.where(visible, jnp.exp2(scores - stats[0, half : half + 1, :]), 0.0)
        grad = dot(v_part, g_part, (1, 1)) - stats[0, 2 + half : 3 + half, :]
        score_low = (attend * grad).astype(BF16)
        diag[half, :, :width] = dot(score_low, q_part, (1, 0))
        diag[half, :, width:] = dot(attend.astype(BF16), g_part, (1, 0))
        dq_acc[0, half * width : (half + 1) * width, :] = dot(k_part, score_low, (0, 0))
    dq_acc[1] = jnp.zeros((2 * width, cols), F32)

    for plane in range(planes):
        for peer in range(inner):
            at = 2 * rank(plane, peer)
            low = jnp.minimum(order[at], order[at + 1])
            low_pos[plane, peer * span : (peer + 1) * span, :] = jnp.full((span, width), low, jnp.int32)

    for index, ref in enumerate((q2, g2, stats)):
        exchange(ref, index).wait_recv()

    def send_part(plane, step):
        peer = peer_of(step)
        return pltpu.make_async_remote_copy(
            src_ref=part_send.at[plane, :, pl.ds(pl.multiple_of(peer * span, span), span), :],
            dst_ref=part_recv.at[plane, i],
            send_sem=s_part.at[plane, step], recv_sem=r_part.at[plane, i],
            device_id=beside(peer), device_id_type=MESH,
        )

    def gather_part(plane):
        total = own[plane]
        for step in range(1, inner):
            peer = peer_of(step)
            pltpu.make_async_remote_copy(
                src_ref=part_recv.at[plane, peer], dst_ref=part_recv.at[plane, peer],
                send_sem=s_part.at[plane, 0], recv_sem=r_part.at[plane, peer],
                device_id=partner, device_id_type=MESH,
            ).wait_recv()
            total = total + part_recv[plane, peer].astype(F32)
        return total

    def send_plane(step):
        plane = plane_of(step)
        return pltpu.make_async_remote_copy(
            src_ref=z_send.at[plane], dst_ref=z_recv.at[z],
            send_sem=s_z.at[step], recv_sem=r_z.at[z],
            device_id=column(plane), device_id_type=MESH,
        )

    def pass_on(step):
        plane = plane_of(step)
        z_send[plane] = gather_part(plane).astype(BF16)
        send_plane(step).start()

    def one_plane(step, carried):
        plane = plane_of(step)
        for t in rows_of:
            wait_cross(plane, cross[t], 0)
            wait_cross(plane, cross[t], 1)
        k_l, v_l = kv[plane, 0, :, :width], kv[plane, 0, :, width:]
        k_h, v_h = kv[plane, 1, :, :width], kv[plane, 1, :, width:]
        pos = low_pos[plane]
        wide_pos = jnp.concatenate([pos] * (cols // width), axis=1)
        dk_l = dv_l = dk_h = dv_h = None
        for j, edge in ((0, my_low), (1, other_low)):
            def below(x):
                return jnp.where(pos < edge, x, 0.0)

            def above(x):
                return jnp.where(pos > edge, x, 0.0)

            def chosen(low, high):
                low, high = below(low.astype(F32)), above(high.astype(F32))
                return jnp.concatenate([low.astype(BF16), high.astype(BF16)], axis=1)

            q_both, g_both = q2[j], g2[j]
            q_h, g_h = q_both[:, width:], g_both[:, width:]
            lse_l, lse_h = stats[j, 0:1, :], stats[j, 1:2, :]
            del_l, del_h = stats[j, 2:3, :], stats[j, 3:4, :]
            attend = jnp.exp2(dot(k_l, q_h, (1, 1)) * (scale * LOG2E) - lse_h)
            score_low = (attend * (dot(v_l, g_h, (1, 1)) - del_h)).astype(BF16)
            dv1 = dot(attend.astype(BF16), g_h, (1, 0))
            dk1 = dot(score_low, q_h, (1, 0))
            dq_acc[j, width:, :] += dot(k_l, score_low, (0, 0))
            is_below = wide_pos < edge
            k_c, v_c = chosen(k_l, k_h), chosen(v_l, v_h)
            attend = jnp.exp2(
                dot(k_c, q_both, (1, 1)) * (scale * LOG2E) - jnp.where(is_below, lse_l, lse_h)
            )
            grad = dot(v_c, g_both, (1, 1)) - jnp.where(is_below, del_l, del_h)
            score_low = (attend * grad).astype(BF16)
            dv2 = dot(attend.astype(BF16), g_both, (1, 0))
            dk2 = dot(score_low, q_both, (1, 0))
            dq_acc[j] += dot(k_c, score_low, (0, 0))
            dk_lj, dk_hj = dk1 + below(dk2[:, :width]), above(dk2[:, width:])
            dv_lj, dv_hj = dv1 + below(dv2[:, :width]), above(dv2[:, width:])
            if j == 0:
                dk_l, dk_h, dv_l, dv_h = dk_lj, dk_hj, dv_lj, dv_hj

                @pl.when(step + 1 < planes)
                def _():
                    forward(plane_of(step + 1))
            else:
                dk_l, dk_h, dv_l, dv_h = dk_l + dk_lj, dk_h + dk_hj, dv_l + dv_lj, dv_h + dv_hj
        for half, dk, dv in ((0, dk_l, dv_l), (1, dk_h, dv_h)):
            full[half, :, :width] = dk
            full[half, :, width:] = dv
            part_send[plane, half, :, :width] = dk.astype(BF16)
            part_send[plane, half, :, width:] = dv.astype(BF16)
        own[plane] = full[:, mine, :]
        for hop in range(1, inner):
            send_part(plane, hop).start()

        @pl.when(step >= 2)
        def _():
            pass_on(step - 1)

        return carried

    lax.fori_loop(0, planes, one_plane, 0)

    dq_send[...] = dq_acc[1].astype(BF16)
    dq_copy = pltpu.make_async_remote_copy(
        src_ref=dq_send, dst_ref=dq_recv, send_sem=s_dq, recv_sem=r_dq,
        device_id=partner, device_id_type=MESH,
    )
    dq_copy.start()
    pass_on(planes - 1)

    dq_copy.wait_recv()
    dq = (dq_acc[0] + dq_recv[...].astype(F32)) * scale
    for at, part in zip((0, span), ordered(dq[:width], dq[width:])):
        dq_out[:, at : at + span, :] = part.T.astype(BF16).reshape(heads, span, width)

    total = gather_part(z) + diag[...]
    for step in range(1, planes):
        plane = plane_of(step)
        pltpu.make_async_remote_copy(
            src_ref=z_recv.at[plane], dst_ref=z_recv.at[plane],
            send_sem=s_z.at[0], recv_sem=r_z.at[plane],
            device_id=partner, device_id_type=MESH,
        ).wait_recv()
        total = total + z_recv[plane].astype(F32)
    for at, part in zip((0, span), ordered(total[0], total[1])):
        dk_out[at : at + span, :] = (part[:, :width] * scale).astype(BF16)
        dv_out[at : at + span, :] = part[:, width:].astype(BF16)

    for step in range(1, planes):
        send_column(step).wait_send()
        send_plane(step).wait_send()
    for step in range(planes):
        for hop in range(1, inner):
            send_part(plane_of(step), hop).wait_send()
        for t in range(inner // 2):
            send_beside(plane_of(step), t).wait_send()
        for t in rows_of:
            send_cross(plane_of(step), t, 0).wait_send()
            send_cross(plane_of(step), t, 1).wait_send()
    for index, ref in enumerate((q2, g2, stats)):
        exchange(ref, index).wait_send()
    dq_copy.wait_send()


def body(queries, key_states, value_states, outputs, grad_outputs, log_sums, span_order):
    heads, rows, width = queries.shape
    planes = lax.axis_size("outer") // 2
    inner = lax.axis_size("inner")
    span = rows // 2
    cols = heads * span
    group = inner * span
    vmem = pl.BlockSpec(memory_space=pltpu.VMEM)
    dma = pltpu.SemaphoreType.DMA
    return pl.pallas_call(
        functools.partial(kernel, planes, inner),
        out_shape=(
            jax.ShapeDtypeStruct(queries.shape, BF16),
            jax.ShapeDtypeStruct(key_states.shape, BF16),
            jax.ShapeDtypeStruct(value_states.shape, BF16),
        ),
        in_specs=[pl.BlockSpec(memory_space=pl.ANY)] * 7,
        out_specs=(vmem, vmem, vmem),
        scratch_shapes=[
            pltpu.VMEM((planes, 2, group, 2 * width), BF16),
            pltpu.VMEM((2, cols, 2 * width), BF16),
            pltpu.VMEM((2, cols, 2 * width), BF16),
            pltpu.VMEM((2, 8, cols), F32),
            pltpu.VMEM((planes, group, width), jnp.int32),
            pltpu.VMEM((2, 2 * width, cols), F32),
            pltpu.VMEM((2 * width, cols), BF16),
            pltpu.VMEM((2 * width, cols), BF16),
            pltpu.VMEM((2, span, 2 * width), F32),
            pltpu.VMEM((2, group, 2 * width), F32),
            pltpu.VMEM((planes, 2, span, 2 * width), F32),
            pltpu.VMEM((planes, 2, group, 2 * width), BF16),
            pltpu.VMEM((planes, inner, 2, span, 2 * width), BF16),
            pltpu.VMEM((planes, 2, span, 2 * width), BF16),
            pltpu.VMEM((planes, 2, span, 2 * width), BF16),
            pltpu.SMEM(span_order.shape, jnp.int32),
            pltpu.VMEM(queries.shape, BF16), pltpu.VMEM(key_states.shape, BF16),
            pltpu.VMEM(value_states.shape, BF16), pltpu.VMEM(outputs.shape, BF16),
            pltpu.VMEM(grad_outputs.shape, BF16), pltpu.VMEM(log_sums.shape, F32),
            dma((7,)),
            dma((planes,)), dma((planes, inner)), dma((planes, inner)),
            dma((planes, inner, 2)), dma((planes, inner, 2)),
            dma((3,)), dma((3,)),
            dma((planes, inner)), dma((planes, inner)),
            dma((planes,)), dma((planes,)),
            dma, dma,
        ],
        compiler_params=pltpu.CompilerParams(
            collective_id=0, has_side_effects=True, vmem_limit_bytes=48 * 1024 * 1024
        ),
        cost_estimate=pl.CostEstimate(
            flops=10 * 65 * cols * span * width * planes * inner // 16,
            bytes_accessed=4 * heads * rows * width * 2,
            transcendentals=0,
        ),
    )(span_order, queries, key_states, value_states, outputs, grad_outputs, log_sums)


def solution(mesh):
    return jax.shard_map(
        body,
        mesh=mesh,
        in_specs=(
            P(None, ("outer", "inner"), None),
            P(("outer", "inner"), None),
            P(("outer", "inner"), None),
            P(None, ("outer", "inner"), None),
            P(None, ("outer", "inner"), None),
            P(None, ("outer", "inner")),
            P(),
        ),
        out_specs=(
            P(None, ("outer", "inner"), None),
            P(("outer", "inner"), None),
            P(("outer", "inner"), None),
        ),
        check_vma=False,
    )
```
